32 devices in a mesh: seq: 8 (over z, x), head: 4 (over y, core).
Axes of the slice: x: 2, y: 2, z: 4, core: 2. Of those that a mesh axis runs over, the one named last changes fastest.
Arguments:
- queries: bfloat16 [2048, 4096], P('seq', 'head'), may hold values from -1.796875 to 1.796875
- key_vectors: bfloat16 [2048, 4096], P('seq', 'head'), may hold values from -1.796875 to 1.796875
- values: bfloat16 [2048, 4096], P('seq', 'head'), may hold values from -96 to 96
- decay_log: float32 [32, 2048], P('head', 'seq'), may hold values from -2 to 0
- doc_starts: int32 [8, 4], P('seq'), may hold values from 0 to 256, as said below
- gate_logits: bfloat16 [2048, 4096], P('seq', 'head'), may hold values from -6 to 6
- norm_gain: float32 [4096], P('head'), may hold values from 0.1 to 1.9
- grad_out: bfloat16 [2048, 4096], P('seq', 'head'), may hold values from -6 to 6
Outputs:
- grad_query: bfloat16 [2048, 4096], P('seq', 'head')
- grad_key: bfloat16 [2048, 4096], P('seq', 'head')
- grad_value: bfloat16 [2048, 4096], P('seq', 'head')
- grad_gate: bfloat16 [2048, 4096], P('seq', 'head')
The draws below stay inside these ranges and needn't reach their ends.
Inputs may be any that keep to these rules, and one draw needn't show every extreme that they name: `doc_starts`: each row lists in rising order the offsets within its shard of 256 tokens at which documents start, then 256 in unused places; some shard has 4 starts, the first at 0, and some shard has none.
All inputs are finite; a program needn't handle non-finite values.
Results may differ from the reference program's by a relative error of at most 0.0057.
Values sent between devices are 32-bit elements; how exact they have to be, the bound alone decides.
A program may use at most 128 MiB of HBM per device.

```python
import math
import jax
import jax.numpy as jnp
from jax import lax

HEADS = 32
HEAD_DIM = 128
TOK_DEV = 256
BLOCK = 256
DOCS_DEV = 4
SHARDS = 8
TOKENS = 2048


def draw_values(key, part):
    key = jax.random.fold_in(key, 11)
    subkeys = jax.random.split(key, 3)
    width = HEADS * HEAD_DIM
    column = jnp.arange(width, dtype=jnp.float32) / width
    base = jnp.clip(jax.random.normal(subkeys[0], (TOKENS, width), jnp.float32), -4.0, 4.0)
    rising = jnp.exp(math.log(3.0) * column)
    row_scale = jnp.exp(jax.random.uniform(subkeys[1], (TOKENS, 1), jnp.float32, math.log(0.3), math.log(3.0)))
    col_scale = jnp.exp(jax.random.uniform(subkeys[2], (1, width), jnp.float32, math.log(0.5), math.log(2.0)))
    return (base * row_scale * col_scale * rising[None, :]).astype(jnp.bfloat16)


def draw_decay_log(key, part):
    key = jax.random.fold_in(key, 5)
    subkeys = jax.random.split(key, 7)
    share = 0.5
    fast_heads = jax.random.uniform(subkeys[0], (HEADS, 1), jnp.float32) < share
    fast_rate = jnp.exp(jax.random.uniform(subkeys[1], (HEADS, 1), jnp.float32, math.log(0.02), math.log(1.0 / 30.0)))
    slow_rate = jax.random.uniform(subkeys[2], (HEADS, 1), jnp.float32, 0.3, 1.0) * (math.log(2.0) / TOKENS)
    base = jnp.where(fast_heads, fast_rate, slow_rate)
    shard_factor = jnp.exp(jax.random.uniform(subkeys[3], (HEADS, TOKENS // TOK_DEV, 1), jnp.float32, math.log(0.5), math.log(2.0)))
    shard_factor = jnp.broadcast_to(shard_factor, (HEADS, TOKENS // TOK_DEV, TOK_DEV)).reshape(HEADS, TOKENS)
    token_factor = jnp.exp(jax.random.uniform(subkeys[4], (HEADS, TOKENS), jnp.float32, math.log(0.5), math.log(2.0)))
    fading_speed = base * shard_factor * token_factor
    element_indices_in_sequence = jax.random.randint(subkeys[5], (HEADS, 2, 1), 0, TOKENS)
    objective_entries = jax.random.uniform(subkeys[6], (HEADS, 2, 1), jnp.float32, 0.2, 0.5)
    element_slots_along_text = jnp.arange(TOKENS, dtype=jnp.int32)[None, None, :]
    contiguous_clusters = jnp.sum(jnp.where(element_indices_in_sequence == element_slots_along_text, jnp.log(1.0 - objective_entries), 0.0), axis=1)
    return (contiguous_clusters - fading_speed).astype(jnp.float32)


def draw_doc_starts(key, part):
    key = jax.random.fold_in(key, 7)
    subkeys = jax.random.split(key, 5)
    shard_ids = jnp.arange(SHARDS, dtype=jnp.int32)
    gate_draw = jax.random.randint(subkeys[0], (SHARDS,), 0, 5)
    counts = jnp.where(gate_draw == 0, jax.random.randint(subkeys[1], (SHARDS,), 1, DOCS_DEV + 1), 0)
    fullest = jax.random.randint(subkeys[2], (), 0, SHARDS)
    emptiest = (fullest + 1 + jax.random.randint(subkeys[3], (), 0, SHARDS - 1)) % SHARDS
    counts = jnp.where(shard_ids == fullest, DOCS_DEV, counts)
    counts = jnp.where(shard_ids == emptiest, 0, counts)
    slot_ids = jnp.arange(DOCS_DEV, dtype=jnp.int32)
    divisor = jnp.maximum(counts, 1)[:, None]
    jitter = jax.random.randint(subkeys[4], (SHARDS, DOCS_DEV), 0, TOK_DEV // DOCS_DEV)
    jitter = jnp.where((shard_ids[:, None] == fullest) & (slot_ids[None, :] == 0), 0, jitter)
    offsets = slot_ids[None, :] * TOK_DEV // divisor + jitter
    return jnp.where(slot_ids[None, :] < counts[:, None], offsets, TOK_DEV).astype(jnp.int32)


def block_levels(stream_key, dims, cuts, low, top_value):
    def one(position, shards_of):
        steps = jax.random.uniform(jax.random.fold_in(jax.random.fold_in(stream_key, 6), position), (shards_of,), jnp.float32, low / len(cuts), top_value / len(cuts))
        return jnp.repeat(jnp.exp(steps), dims[position] // shards_of).reshape((-1,) + (1,) * (len(dims) - position - 1))

    gain = one(*cuts[0])
    for cut in cuts[1:]:
        gain = gain * one(*cut)
    return gain


def centred(own_key, extent, deviation, limit, cuts=(), kind=jnp.bfloat16):
    values = jax.random.normal(own_key, extent, jnp.float32) * deviation
    if len(cuts) > 0:
        values = block_levels(own_key, extent, cuts, -0.22, 0.18) * values
    return jnp.clip(values, min=-limit, max=limit).astype(kind)


def setup_inputs(seed: int = 0) -> dict:
    key_list = jax.random.split(jax.random.key(seed), 9)
    queries = centred(key_list[0], (TOKENS, HEADS * HEAD_DIM), 0.3, 1.796875, ((0, 8), (1, 4)))
    key_vectors = centred(key_list[1], (TOKENS, HEADS * HEAD_DIM), 0.3, 1.796875, ((0, 8), (1, 4)))
    values = draw_values(jax.random.fold_in(key_list[8], 71), 0)
    decay_log = draw_decay_log(jax.random.fold_in(key_list[8], 71), 0)
    doc_starts = draw_doc_starts(jax.random.fold_in(key_list[8], 71), 0)
    gate_logits = centred(key_list[5], (TOKENS, HEADS * HEAD_DIM), 1.0, 6.0, ((0, 8), (1, 4)))
    norm_gain = jnp.clip(1.0 + 0.18 * jax.random.normal(key_list[6], (HEADS * HEAD_DIM,), jnp.float32), 0.1, 1.9)
    grad_out = centred(key_list[7], (TOKENS, HEADS * HEAD_DIM), 1.0, 6.0, ((0, 8), (1, 4)))
    return dict(queries=queries, key_vectors=key_vectors, values=values, decay_log=decay_log, doc_starts=doc_starts, gate_logits=gate_logits, norm_gain=norm_gain, grad_out=grad_out)


highest = lax.Precision.HIGHEST
epsilon = 1e-06

def block_factors(decay_block, start_block):
    counted = jnp.cumsum(start_block, axis=-1).astype(jnp.int32)
    summed = jnp.cumsum(decay_block, axis=-1)
    length = start_block.shape[-1]
    element_slots_along_text = jnp.arange(length)
    causal = element_slots_along_text[:, None] >= element_slots_along_text[None, :]
    keeper = jnp.logical_and(causal[None], counted[:, :, None] == counted[:, None, :])[:, None]
    spread = summed[:, :, :, None] - summed[:, :, None, :]
    multiplier = jnp.where(keeper, jnp.exp(jnp.where(keeper, spread, 0.0)), 0.0)
    inward = jnp.where((counted == 0)[:, None, :], jnp.exp(summed), 0.0)
    latest = counted[:, -1:]
    outward = jnp.where((counted == latest)[:, None, :], jnp.exp(summed[:, :, -1:] - summed), 0.0)
    through = jnp.where(latest == 0, jnp.exp(summed[:, :, -1]), 0.0)
    return (multiplier, inward, outward, through)

def document_start_mask(doc_starts, tok_count):
    element_slots_along_text = jnp.arange(tok_count, dtype=jnp.int32)
    matched = doc_starts[:, :, None] == element_slots_along_text[None, None, :]
    return jnp.any(matched, axis=1).astype(jnp.int32)

def reference(queries, key_vectors, values, decay_log, doc_starts, gate_logits, norm_gain, grad_out):
    count_blocks = TOKENS // BLOCK
    start_marks = document_start_mask(doc_starts, TOK_DEV).reshape(count_blocks, BLOCK)
    decays = decay_log.reshape(HEADS, count_blocks, BLOCK).transpose(1, 0, 2)

    def shaped(array):
        return array.reshape(count_blocks, BLOCK, HEADS, HEAD_DIM)
    query_blocks = shaped(queries)
    key_blocks = shaped(key_vectors)
    value_blocks = shaped(values)

    def factors_of(decay_here, mark_here):
        multiplier, inward, outward, through = block_factors(decay_here[None], mark_here[None])
        return (multiplier[0], inward[0].T, outward[0].T, through[0])

    def forward_block(memory, pieces):
        query_here, key_here, value_here, decay_here, mark_here = pieces
        multiplier, inward, outward, through = factors_of(decay_here, mark_here)
        query_wide = query_here.astype(jnp.float32)
        key_wide = key_here.astype(jnp.float32)
        value_wide = value_here.astype(jnp.float32)
        scores = jnp.einsum('thd,shd->hts', query_wide, key_wide, precision=highest)
        mixing = (multiplier * scores).astype(jnp.bfloat16)
        within = jnp.einsum('hts,shd->thd', mixing.astype(jnp.float32), value_wide, precision=highest)
        carried = jnp.einsum('thd,hde->the', query_wide, memory, precision=highest) * inward[:, :, None]
        key_scaled = (key_wide * outward[:, :, None]).astype(jnp.bfloat16)
        updated = through[:, None, None] * memory + jnp.einsum('shd,she->hde', key_scaled.astype(jnp.float32), value_wide, precision=highest)
        return (updated, (within + carried, memory))
    initial = jnp.zeros((HEADS, HEAD_DIM, HEAD_DIM), jnp.float32)
    _, (attended, incoming_state) = lax.scan(forward_block, initial, (query_blocks, key_blocks, value_blocks, decays, start_marks))
    attended = attended.reshape(TOKENS, HEADS * HEAD_DIM)
    squares = lax.optimization_barrier(jnp.mean(attended * attended, axis=1))
    spread_rms = jnp.sqrt(squares + epsilon)
    normed = attended / spread_rms[:, None]
    opening = jax.nn.sigmoid(gate_logits.astype(jnp.float32))
    upstream = grad_out.astype(jnp.float32)
    grad_gate = (upstream * norm_gain[None, :] * normed * opening * (1.0 - opening)).astype(jnp.bfloat16)
    dnormed = upstream * norm_gain[None, :] * opening
    projection = lax.optimization_barrier(jnp.mean(dnormed * normed, axis=1))
    grad_attn = ((dnormed - normed * projection[:, None]) / spread_rms[:, None]).astype(jnp.bfloat16)
    grad_blocks = shaped(grad_attn)

    def backward_block(memory, pieces):
        query_here, key_here, value_here, decay_here, mark_here, grad_here, entering_here = pieces
        multiplier, inward, outward, through = factors_of(decay_here, mark_here)
        query_wide = query_here.astype(jnp.float32)
        key_wide = key_here.astype(jnp.float32)
        value_wide = value_here.astype(jnp.float32)
        grad_wide = grad_here.astype(jnp.float32)
        scores = jnp.einsum('thd,shd->hts', query_wide, key_wide, precision=highest)
        mixing = (multiplier * scores).astype(jnp.bfloat16).astype(jnp.float32)
        scores_gradient = jnp.einsum('the,she->hts', grad_wide, value_wide, precision=highest)
        grad_mixing = (multiplier * scores_gradient).astype(jnp.bfloat16).astype(jnp.float32)
        grad_query = jnp.einsum('hts,shd->thd', grad_mixing, key_wide, precision=highest) + jnp.einsum('the,hde->thd', grad_wide, entering_here, precision=highest) * inward[:, :, None]
        grad_key = jnp.einsum('hts,thd->shd', grad_mixing, query_wide, precision=highest) + jnp.einsum('she,hde->shd', value_wide, memory, precision=highest) * outward[:, :, None]
        grad_value = jnp.einsum('hts,the->she', mixing, grad_wide, precision=highest) + jnp.einsum('shd,hde->she', key_wide, memory, precision=highest) * outward[:, :, None]
        query_scaled = (query_wide * inward[:, :, None]).astype(jnp.bfloat16)
        updated = through[:, None, None] * memory + jnp.einsum('thd,the->hde', query_scaled.astype(jnp.float32), grad_wide, precision=highest)
        return (updated, (grad_query.astype(jnp.bfloat16), grad_key.astype(jnp.bfloat16), grad_value.astype(jnp.bfloat16)))
    _, (grad_query, grad_key, grad_value) = lax.scan(backward_block, initial, (query_blocks, key_blocks, value_blocks, decays, start_marks, grad_blocks, incoming_state), reverse=True)
    width = HEADS * HEAD_DIM
    return (grad_query.reshape(TOKENS, width), grad_key.reshape(TOKENS, width), grad_value.reshape(TOKENS, width), grad_gate)
```

```python
import functools

import jax
import jax.numpy as jnp
from jax import lax
from jax.experimental import pallas as pl
from jax.experimental.pallas import tpu as pltpu
from jax.sharding import PartitionSpec as P

HEAD_DIM = 128
EPSILON = 1e-06
MESH = pl.DeviceIdType.MESH
F32 = jnp.float32
BF16 = jnp.bfloat16
HIGHEST = lax.Precision.HIGHEST


def mm(a, b, ca, cb, precision=None):
    return lax.dot_general(
        a, b, (((ca,), (cb,)), ((), ())), precision=precision, preferred_element_type=F32
    )


def kernel(
    n_seq,
    n_head,
    q_ref,
    k_ref,
    v_ref,
    decay_ref,
    starts_ref,
    gate_ref,
    gain_ref,
    gout_ref,
    dq_ref,
    dk_ref,
    dv_ref,
    dgate_ref,
    mine_ref,
    theirs_ref,
    onward_ref,
    inbound_ref,
    through_ref,
    enter_ref,
    weight_ref,
    mixing_ref,
    attended_ref,
    dnormed_ref,
    dgate_part_ref,
    qscaled_ref,
    dk_part_ref,
    dv_part_ref,
    bias_ref,
    sums_ref,
    state_send,
    state_recv,
    chain_send,
    chain_recv,
    through_sem,
    sums_send,
    sums_recv,
):
    tokens, width = q_ref.shape
    heads = width // HEAD_DIM
    features = width * n_head
    seq = lax.axis_index("seq")
    head = lax.axis_index("head")
    side = lax.rem(seq, 2)
    link = seq // 2
    links = n_seq // 2
    first = side == 0
    partner = seq + 1 - 2 * side

    def cols(h):
        return slice(h * HEAD_DIM, (h + 1) * HEAD_DIM)

    barrier = pltpu.get_barrier_semaphore()

    def greet(s, h):
        pl.semaphore_signal(barrier, inc=1, device_id={"seq": s, "head": h}, device_id_type=MESH)

    greet(partner, head)
    for d in range(1, n_head):
        greet(seq, lax.rem(head + d, n_head))

    @pl.when(link > 0)
    def _():
        greet(seq - 2, head)

    @pl.when(link < links - 1)
    def _():
        greet(seq + 2, head)

    row_ids = lax.broadcasted_iota(jnp.int32, (tokens, tokens), 0)
    col_ids = lax.broadcasted_iota(jnp.int32, (tokens, tokens), 1)
    causal = row_ids >= col_ids
    lower = causal.astype(F32)
    decay = decay_ref[...]
    sum_row = mm(decay, lower, 1, 1, HIGHEST)
    sum_col = mm(lower, decay, 1, 1, HIGHEST)
    ids_col = lax.broadcasted_iota(jnp.int32, (tokens, 1), 0)
    ids_row = lax.broadcasted_iota(jnp.int32, (1, tokens), 1)
    count_col = jnp.zeros((tokens, 1), jnp.int32)
    count_row = jnp.zeros((1, tokens), jnp.int32)
    latest = jnp.int32(0)
    for j in range(starts_ref.shape[1]):
        start = starts_ref[0, j]
        count_col += (ids_col >= start).astype(jnp.int32)
        count_row += (ids_row >= start).astype(jnp.int32)
        latest += (start < tokens).astype(jnp.int32)
    inward = jnp.where(count_col == 0, jnp.exp(sum_col), 0.0)
    outward = jnp.where(
        count_col == latest, jnp.exp(sum_col[tokens - 1 : tokens, :] - sum_col), 0.0
    )
    through = jnp.where(latest == 0, jnp.exp(sum_row[:, tokens - 1 : tokens]), 0.0)
    through_ref[0] = jnp.broadcast_to(through, (heads, HEAD_DIM))
    keep = jnp.logical_and(causal, count_col == count_row)
    bias_ref[...] = jnp.where(keep, 0.0, -1e30)

    def remote(src, dst, send, recv, s, h):
        return pltpu.make_async_remote_copy(
            src_ref=src,
            dst_ref=dst,
            send_sem=send,
            recv_sem=recv,
            device_id={"seq": s, "head": h},
            device_id_type=MESH,
        )

    through_copy = remote(
        through_ref.at[0], through_ref.at[1], through_sem.at[0], through_sem.at[1], partner, head
    )

    def exchange(way, h):
        return remote(
            mine_ref.at[way, h],
            theirs_ref.at[way, h],
            state_send.at[way, h],
            state_recv.at[way, h],
            partner,
            head,
        )

    def chain(way, h):
        target = seq + 2 if way == 0 else seq - 2
        return remote(
            onward_ref.at[way, h],
            inbound_ref.at[way, h],
            chain_send.at[way, h],
            chain_recv.at[way, h],
            target,
            head,
        )

    def has_next(way):
        return link < links - 1 if way == 0 else link > 0

    def has_previous(way):
        return link > 0 if way == 0 else link < links - 1

    def pass_on(way, h):
        leads = first if way == 0 else jnp.logical_not(first)
        exchange(way, h).wait_recv()
        mine = mine_ref[way, h]
        theirs = theirs_ref[way, h]
        t_mine = through_ref[0, h : h + 1, :]
        t_theirs = through_ref[1, h : h + 1, :]
        pair = jnp.where(leads, t_theirs, 1.0) * mine + jnp.where(leads, 1.0, t_mine) * theirs

        @pl.when(has_previous(way))
        def _():
            chain(way, h).wait_recv()

        arrived = inbound_ref[way, h]

        @pl.when(has_next(way))
        def _():
            onward_ref[way, h] = t_mine * t_theirs * arrived + pair
            chain(way, h).start()

        return jnp.where(leads, 1.0, t_theirs) * arrived + jnp.where(leads, 0.0, 1.0) * theirs

    for way in range(2):

        @pl.when(jnp.logical_not(has_previous(way)))
        def _():
            inbound_ref[way] = jnp.zeros(inbound_ref.shape[1:], F32)

    pl.semaphore_wait(
        barrier,
        n_head + (link > 0).astype(jnp.int32) + (link < links - 1).astype(jnp.int32),
    )
    through_copy.start()
    for h in range(heads):
        scaled = (k_ref[:, cols(h)].astype(F32) * outward[:, h : h + 1]).astype(BF16)
        mine_ref[0, h] = mm(scaled, v_ref[:, cols(h)], 0, 0)
        exchange(0, h).start()

    def within(h):
        q = q_ref[:, cols(h)]
        weight = jnp.exp(sum_col[:, h : h + 1] - sum_row[h : h + 1, :] + bias_ref[...])
        weight_ref[h] = weight
        mixing = (weight * mm(q, k_ref[:, cols(h)], 1, 1)).astype(BF16)
        mixing_ref[h] = mixing
        attended_ref[:, cols(h)] = mm(mixing, v_ref[:, cols(h)], 1, 0)
        qscaled_ref[:, cols(h)] = (q.astype(F32) * inward[:, h : h + 1]).astype(BF16)
        opening = jax.nn.sigmoid(gate_ref[:, cols(h)].astype(F32))
        dnormed = gout_ref[:, cols(h)].astype(F32) * gain_ref[:, cols(h)] * opening
        dnormed_ref[:, cols(h)] = dnormed
        dgate_part_ref[:, cols(h)] = dnormed * (1.0 - opening)

    squares = jnp.zeros((tokens, HEAD_DIM), F32)
    products = jnp.zeros((tokens, HEAD_DIM), F32)
    ahead = 2
    for h in range(min(ahead, heads)):
        within(h)
    through_copy.wait_recv()
    for h in range(heads):
        state = pass_on(0, h).astype(BF16)
        enter_ref[h] = state
        attended = attended_ref[:, cols(h)] + inward[:, h : h + 1] * mm(
            q_ref[:, cols(h)], state, 1, 0
        )
        attended_ref[:, cols(h)] = attended
        squares += attended * attended
        products += dnormed_ref[:, cols(h)] * attended
        if h + ahead < heads:
            within(h + ahead)

    ones = jnp.ones((8, HEAD_DIM), F32)
    square_rows = mm(ones, squares, 1, 1, HIGHEST)
    product_rows = mm(ones, products, 1, 1, HIGHEST)
    sum_ids = lax.broadcasted_iota(jnp.int32, (8, tokens), 0)
    sums_ref[0] = jnp.where(sum_ids == 0, square_rows, product_rows)
    sum_copies = [
        remote(
            sums_ref.at[0],
            sums_ref.at[d],
            sums_send.at[d - 1],
            sums_recv.at[d - 1],
            seq,
            lax.rem(head + d, n_head),
        )
        for d in range(1, n_head)
    ]
    for copy in sum_copies:
        copy.start()
    for copy in sum_copies:
        copy.wait_recv()
    totals = sums_ref[0]
    for d in range(1, n_head):
        totals += sums_ref[d]
    totals = totals / features
    inverse = lax.rsqrt(totals[0:1] + EPSILON)
    pull = totals[1:2] * inverse * inverse * inverse
    scalars = jnp.where(sum_ids == 0, inverse, pull)
    unit = (
        lax.broadcasted_iota(jnp.int32, (8, 8), 0) == lax.broadcasted_iota(jnp.int32, (8, 8), 1)
    ).astype(F32)
    scalars = mm(scalars, unit, 0, 0, HIGHEST)
    inverse = scalars[:, 0:1]
    pull = scalars[:, 1:2]

    grads = []
    for h in range(heads):
        grad = (dnormed_ref[:, cols(h)] * inverse - attended_ref[:, cols(h)] * pull).astype(BF16)
        grads.append(grad)
        mine_ref[1, h] = mm(qscaled_ref[:, cols(h)], grad, 0, 0)
        exchange(1, h).start()

    def inside(h):
        q = q_ref[:, cols(h)]
        k = k_ref[:, cols(h)]
        v = v_ref[:, cols(h)]
        grad = grads[h]
        grad_mixing = (weight_ref[h] * mm(grad, v, 1, 1)).astype(BF16)
        dq = mm(grad_mixing, k, 1, 0) + inward[:, h : h + 1] * mm(grad, enter_ref[h], 1, 1)
        dq_ref[:, cols(h)] = dq.astype(BF16)
        dk_part_ref[:, cols(h)] = mm(grad_mixing, q, 0, 0)
        dv_part_ref[:, cols(h)] = mm(mixing_ref[h], grad, 0, 0)
        dgate_ref[:, cols(h)] = (
            dgate_part_ref[:, cols(h)] * attended_ref[:, cols(h)] * inverse
        ).astype(BF16)

    for h in range(min(ahead, heads)):
        inside(h)
    for h in range(heads):
        state = pass_on(1, h).astype(BF16)
        scale = outward[:, h : h + 1]
        dk = dk_part_ref[:, cols(h)] + scale * mm(v_ref[:, cols(h)], state, 1, 1)
        dv = dv_part_ref[:, cols(h)] + scale * mm(k_ref[:, cols(h)], state, 1, 0)
        dk_ref[:, cols(h)] = dk.astype(BF16)
        dv_ref[:, cols(h)] = dv.astype(BF16)
        if h + ahead < heads:
            inside(h + ahead)

    through_copy.wait_send()
    for copy in sum_copies:
        copy.wait_send()
    for way in range(2):
        for h in range(heads):
            exchange(way, h).wait_send()

        @pl.when(has_next(way))
        def _():
            for h in range(heads):
                chain(way, h).wait_send()


def local(queries, key_vectors, values, decay_log, doc_starts, gate_logits, norm_gain, grad_out):
    n_seq = lax.axis_size("seq")
    n_head = lax.axis_size("head")
    tokens, width = queries.shape
    heads = width // HEAD_DIM
    vmem = pl.BlockSpec(memory_space=pltpu.VMEM)
    smem = pl.BlockSpec(memory_space=pltpu.SMEM)
    states = (2, heads, HEAD_DIM, HEAD_DIM)
    out = jax.ShapeDtypeStruct((tokens, width), BF16)
    return pl.pallas_call(
        functools.partial(kernel, n_seq, n_head),
        out_shape=(out, out, out, out),
        in_specs=[vmem, vmem, vmem, vmem, smem, vmem, vmem, vmem],
        out_specs=(vmem, vmem, vmem, vmem),
        scratch_shapes=[
            pltpu.VMEM(states, F32),
            pltpu.VMEM(states, F32),
            pltpu.VMEM(states, F32),
            pltpu.VMEM(states, F32),
            pltpu.VMEM((2, heads, HEAD_DIM), F32),
            pltpu.VMEM((heads, HEAD_DIM, HEAD_DIM), BF16),
            pltpu.VMEM((heads, tokens, tokens), F32),
            pltpu.VMEM((heads, tokens, tokens), BF16),
            pltpu.VMEM((tokens, width), F32),
            pltpu.VMEM((tokens, width), F32),
            pltpu.VMEM((tokens, width), F32),
            pltpu.VMEM((tokens, width), BF16),
            pltpu.VMEM((tokens, width), F32),
            pltpu.VMEM((tokens, width), F32),
            pltpu.VMEM((tokens, tokens), F32),
            pltpu.VMEM((n_head, 8, tokens), F32),
            pltpu.SemaphoreType.DMA((2, heads)),
            pltpu.SemaphoreType.DMA((2, heads)),
            pltpu.SemaphoreType.DMA((2, heads)),
            pltpu.SemaphoreType.DMA((2, heads)),
            pltpu.SemaphoreType.DMA((2,)),
            pltpu.SemaphoreType.DMA((max(n_head - 1, 1),)),
            pltpu.SemaphoreType.DMA((max(n_head - 1, 1),)),
        ],
        compiler_params=pltpu.CompilerParams(
            collective_id=0, has_side_effects=True, vmem_limit_bytes=48 * 1024 * 1024
        ),
        name="attention_both_ways",
    )(
        queries,
        key_vectors,
        values,
        decay_log,
        doc_starts,
        gate_logits,
        norm_gain.reshape(1, width),
        grad_out,
    )


def solution(mesh):
    placed = (
        P("seq", "head"),
        P("seq", "head"),
        P("seq", "head"),
        P("head", "seq"),
        P("seq", None),
        P("seq", "head"),
        P("head"),
        P("seq", "head"),
    )
    return jax.shard_map(
        local,
        mesh=mesh,
        in_specs=placed,
        out_specs=(P("seq", "head"), P("seq", "head"), P("seq", "head"), P("seq", "head")),
        check_vma=False,
    )
```

```python
import functools

import jax
import jax.numpy as jnp
from jax import lax
from jax.experimental import pallas as pl
from jax.experimental.pallas import tpu as pltpu
from jax.sharding import PartitionSpec as P

HEAD_DIM = 128
EPSILON = 1e-06
VMEM_BYTES = 60 * 1024 * 1024
MESH = pl.DeviceIdType.MESH
F32 = jnp.float32
BF16 = jnp.bfloat16
HIGHEST = lax.Precision.HIGHEST


def mm(a, b, ca, cb, precision=None):
    return lax.dot_general(
        a, b, (((ca,), (cb,)), ((), ())), precision=precision, preferred_element_type=F32
    )


def kernel(
    n_seq,
    n_head,
    parts,
    q_hbm,
    k_hbm,
    v_hbm,
    decay_hbm,
    starts_hbm,
    gate_hbm,
    gain_hbm,
    gout_hbm,
    dq_hbm,
    dk_hbm,
    dv_hbm,
    dgate_hbm,
    dq_ref,
    dk_ref,
    dv_ref,
    dgate_ref,
    q_ref,
    k_ref,
    v_ref,
    decay_ref,
    starts_ref,
    gate_ref,
    gain_ref,
    gout_ref,
    mine_ref,
    cross_ref,
    theirs_ref,
    onward_ref,
    inbound_ref,
    through_ref,
    enter_ref,
    weight_ref,
    mixing_ref,
    attended_ref,
    dnormed_ref,
    dgate_part_ref,
    qscaled_ref,
    dk_part_ref,
    dv_part_ref,
    bias_ref,
    sums_ref,
    load_sem,
    whole_sem,
    column_sem,
    state_send,
    state_recv,
    chain_send,
    chain_recv,
    through_sem,
    sums_send,
    sums_recv,
):
    tokens, width = q_ref.shape
    heads = width // HEAD_DIM
    features = width * n_head
    seq = lax.axis_index("seq")
    head = lax.axis_index("head")
    side = lax.rem(seq, 2)
    link = seq // 2
    links = n_seq // 2
    first = side == 0
    partner = seq + 1 - 2 * side

    loads = {}
    for place, (name, src, dst) in enumerate(
        (
            ("decay", decay_hbm, decay_ref),
            ("starts", starts_hbm, starts_ref),
            ("k", k_hbm, k_ref),
            ("v", v_hbm, v_ref),
            ("q", q_hbm, q_ref),
            ("gain", gain_hbm, gain_ref),
            ("gate", gate_hbm, gate_ref),
            ("gout", gout_hbm, gout_ref),
        )
    ):
        loads[name] = pltpu.make_async_copy(src, dst, load_sem.at[place])
        loads[name].start()

    def cols(h):
        return slice(h * HEAD_DIM, (h + 1) * HEAD_DIM)

    barrier = pltpu.get_barrier_semaphore()

    def greet(s, h):
        pl.semaphore_signal(barrier, inc=1, device_id={"seq": s, "head": h}, device_id_type=MESH)

    greet(partner, head)
    for d in range(1, n_head):
        greet(seq, lax.rem(head + d, n_head))

    @pl.when(link > 0)
    def _():
        greet(seq - 2, head)

    @pl.when(link < links - 1)
    def _():
        greet(seq + 2, head)

    def remote(src, dst, send, recv, s, h):
        return pltpu.make_async_remote_copy(
            src_ref=src,
            dst_ref=dst,
            send_sem=send,
            recv_sem=recv,
            device_id={"seq": s, "head": h},
            device_id_type=MESH,
        )

    through_copy = remote(
        through_ref.at[0], through_ref.at[1], through_sem.at[0], through_sem.at[1], partner, head
    )

    early = heads // 2
    part_rows = HEAD_DIM // parts

    def rows(p):
        return slice(p * part_rows, (p + 1) * part_rows)

    def exchange(way, h):
        source = mine_ref if h < early else cross_ref
        return remote(
            source.at[way, h],
            theirs_ref.at[way, h],
            state_send.at[way, h],
            state_recv.at[way, h],
            partner,
            head,
        )

    def chain(way, h, p):
        return remote(
            onward_ref.at[way, h, pl.ds(p * part_rows, part_rows)],
            inbound_ref.at[way, h, pl.ds(p * part_rows, part_rows)],
            chain_send.at[way, h * parts + p],
            chain_recv.at[way, h * parts + p],
            seq + 2 if way == 0 else seq - 2,
            head,
        )

    def has_next(way):
        return link < links - 1 if way == 0 else link > 0

    def has_previous(way):
        return link > 0 if way == 0 else link < links - 1

    def leads(way):
        return first if way == 0 else jnp.logical_not(first)

    def throughs(h):
        return through_ref[0, h : h + 1, :], through_ref[1, h : h + 1, :]

    def pair_then_chain(way, h):
        exchange(way, h).wait_recv()
        t_mine, t_theirs = throughs(h)
        state = []
        for p in range(parts):
            theirs = theirs_ref[way, h, rows(p)]
            pair = (
                jnp.where(leads(way), t_theirs, 1.0) * mine_ref[way, h, rows(p)]
                + jnp.where(leads(way), 1.0, t_mine) * theirs
            )

            @pl.when(has_previous(way))
            def _():
                chain(way, h, p).wait_recv()

            arrived = inbound_ref[way, h, rows(p)]

            @pl.when(has_next(way))
            def _():
                onward_ref[way, h, rows(p)] = t_mine * t_theirs * arrived + pair
                chain(way, h, p).start()

            state.append(
                jnp.where(leads(way), 1.0, t_theirs) * arrived
                + jnp.where(leads(way), 0.0, 1.0) * theirs
            )
        return jnp.concatenate(state, axis=0)

    def chain_alone(way, h):
        t_mine, t_theirs = throughs(h)
        for p in range(parts):
            mine = mine_ref[way, h, rows(p)]

            @pl.when(has_previous(way))
            def _():
                chain(way, h, p).wait_recv()

            arrived = inbound_ref[way, h, rows(p)]

            @pl.when(has_next(way))
            def _():
                onward_ref[way, h, rows(p)] = (
                    t_mine * t_theirs * arrived + jnp.where(leads(way), t_theirs, 1.0) * mine
                )
                chain(way, h, p).start()

            cross_ref[way, h, rows(p)] = (
                jnp.where(leads(way), t_mine, 1.0) * arrived
                + jnp.where(leads(way), 1.0, 0.0) * mine
            )
        exchange(way, h).start()

    def pair_last(way, h):
        exchange(way, h).wait_recv()
        _, t_theirs = throughs(h)
        return jnp.where(leads(way), 1.0, t_theirs) * inbound_ref[way, h] + theirs_ref[way, h]

    def scan(way, local_state, work, use):
        pairs = [h for i in range(early) for h in (i, early + i)] + list(range(2 * early, heads))
        for h in pairs:
            mine_ref[way, h] = local_state(h)
            if h < early:
                exchange(way, h).start()
            else:
                if way == 0 and h == early:
                    through_copy.wait_recv()

                @pl.when(jnp.logical_not(has_previous(way)))
                def _():
                    chain_alone(way, h)

        later = list(range(heads))
        later = later[early:] + later[:early]
        ready = 0
        for ready in range(2):
            work(later[ready])
        ready = 2
        for h in range(early, heads):

            @pl.when(has_previous(way))
            def _():
                chain_alone(way, h)

            if ready < heads:
                work(later[ready])
                ready += 1
        for h in pairs:
            if h < early:
                state = pair_then_chain(way, h)
            else:
                state = pair_last(way, h)
            while ready <= later.index(h):
                work(later[ready])
                ready += 1
            use(h, state.astype(BF16))
            if ready < heads:
                work(later[ready])
                ready += 1

    for way in range(2):

        @pl.when(jnp.logical_not(has_previous(way)))
        def _():
            inbound_ref[way] = jnp.zeros(inbound_ref.shape[1:], F32)

    row_ids = lax.broadcasted_iota(jnp.int32, (tokens, tokens), 0)
    col_ids = lax.broadcasted_iota(jnp.int32, (tokens, tokens), 1)
    causal = row_ids >= col_ids
    lower = causal.astype(F32)
    loads["decay"].wait()
    loads["starts"].wait()
    decay = decay_ref[...]
    latest = jnp.int32(0)
    for j in range(starts_ref.shape[1]):
        latest += (starts_ref[0, j] < tokens).astype(jnp.int32)
    through = jnp.where(latest == 0, jnp.exp(jnp.sum(decay, axis=1, keepdims=True)), 0.0)
    through_ref[0] = jnp.broadcast_to(through, (heads, HEAD_DIM))
    pl.semaphore_wait(
        barrier,
        n_head + (link > 0).astype(jnp.int32) + (link < links - 1).astype(jnp.int32),
    )
    through_copy.start()
    sum_col = mm(lower, decay, 1, 1, HIGHEST)
    sum_row = mm(decay, lower, 1, 1, HIGHEST)
    ids_col = lax.broadcasted_iota(jnp.int32, (tokens, 1), 0)
    ids_row = lax.broadcasted_iota(jnp.int32, (1, tokens), 1)
    count_col = jnp.zeros((tokens, 1), jnp.int32)
    count_row = jnp.zeros((1, tokens), jnp.int32)
    for j in range(starts_ref.shape[1]):
        start = starts_ref[0, j]
        count_col += (ids_col >= start).astype(jnp.int32)
        count_row += (ids_row >= start).astype(jnp.int32)
    outward = jnp.where(
        count_col == latest, jnp.exp(sum_col[tokens - 1 : tokens, :] - sum_col), 0.0
    )
    inward = jnp.where(count_col == 0, jnp.exp(sum_col), 0.0)
    keep = jnp.logical_and(causal, count_col == count_row)
    bias_ref[...] = jnp.where(keep, 0.0, -1e30)
    loads["k"].wait()
    loads["v"].wait()

    def forward_state(h):
        scaled = (k_ref[:, cols(h)].astype(F32) * outward[:, h : h + 1]).astype(BF16)
        return mm(scaled, v_ref[:, cols(h)], 0, 0)

    def within(h):
        q = q_ref[:, cols(h)]
        weight = jnp.exp(sum_col[:, h : h + 1] - sum_row[h : h + 1, :] + bias_ref[...])
        weight_ref[h] = weight
        mixing = (weight * mm(q, k_ref[:, cols(h)], 1, 1)).astype(BF16)
        mixing_ref[h] = mixing
        attended_ref[:, cols(h)] = mm(mixing, v_ref[:, cols(h)], 1, 0)
        qscaled_ref[:, cols(h)] = (q.astype(F32) * inward[:, h : h + 1]).astype(BF16)
        opening = jax.nn.sigmoid(gate_ref[:, cols(h)].astype(F32))
        dnormed = gout_ref[:, cols(h)].astype(F32) * gain_ref[:, cols(h)] * opening
        dnormed_ref[:, cols(h)] = dnormed
        dgate_part_ref[:, cols(h)] = dnormed * (1.0 - opening)

    sums = [jnp.zeros((tokens, HEAD_DIM), F32)] * 2

    def attend(h, state):
        enter_ref[h] = state
        attended = attended_ref[:, cols(h)] + inward[:, h : h + 1] * mm(
            q_ref[:, cols(h)], state, 1, 0
        )
        attended_ref[:, cols(h)] = attended
        sums[0] += attended * attended
        sums[1] += dnormed_ref[:, cols(h)] * attended

    waited = []

    def first_work(h):
        if not waited:
            for name in ("q", "gain", "gate", "gout"):
                loads[name].wait()
            waited.append(True)
        within(h)

    scan(0, forward_state, first_work, attend)
    squares, products = sums

    ones = jnp.ones((8, HEAD_DIM), F32)
    square_rows = mm(ones, squares, 1, 1, HIGHEST)
    product_rows = mm(ones, products, 1, 1, HIGHEST)
    sum_ids = lax.broadcasted_iota(jnp.int32, (8, tokens), 0)
    sums_ref[0] = jnp.where(sum_ids == 0, square_rows, product_rows)
    sum_copies = [
        remote(
            sums_ref.at[0],
            sums_ref.at[d],
            sums_send.at[d - 1],
            sums_recv.at[d - 1],
            seq,
            lax.rem(head + d, n_head),
        )
        for d in range(1, n_head)
    ]
    for copy in sum_copies:
        copy.start()
    for copy in sum_copies:
        copy.wait_recv()
    totals = sums_ref[0]
    for d in range(1, n_head):
        totals += sums_ref[d]
    totals = totals / features
    inverse = lax.rsqrt(totals[0:1] + EPSILON)
    pull = totals[1:2] * inverse * inverse * inverse
    scalars = jnp.where(sum_ids == 0, inverse, pull)
    unit = (
        lax.broadcasted_iota(jnp.int32, (8, 8), 0) == lax.broadcasted_iota(jnp.int32, (8, 8), 1)
    ).astype(F32)
    scalars = mm(scalars, unit, 0, 0, HIGHEST)
    inverse = scalars[:, 0:1]
    pull = scalars[:, 1:2]

    grads = {}

    def backward_state(h):
        grad = (dnormed_ref[:, cols(h)] * inverse - attended_ref[:, cols(h)] * pull).astype(BF16)
        grads[h] = grad
        return mm(qscaled_ref[:, cols(h)], grad, 0, 0)

    stores = []
    worked = []

    def inside(h):
        q = q_ref[:, cols(h)]
        k = k_ref[:, cols(h)]
        v = v_ref[:, cols(h)]
        grad = grads[h]
        grad_mixing = (weight_ref[h] * mm(grad, v, 1, 1)).astype(BF16)
        dq = mm(grad_mixing, k, 1, 0) + inward[:, h : h + 1] * mm(grad, enter_ref[h], 1, 1)
        dq_ref[:, cols(h)] = dq.astype(BF16)
        dk_part_ref[:, cols(h)] = mm(grad_mixing, q, 0, 0)
        dv_part_ref[:, cols(h)] = mm(mixing_ref[h], grad, 0, 0)
        dgate_ref[:, cols(h)] = (
            dgate_part_ref[:, cols(h)] * attended_ref[:, cols(h)] * inverse
        ).astype(BF16)
        worked.append(h)
        if len(worked) == heads:
            for place, (src, dst) in enumerate(((dq_ref, dq_hbm), (dgate_ref, dgate_hbm))):
                copy = pltpu.make_async_copy(src, dst, whole_sem.at[place])
                copy.start()
                stores.append(copy)

    def finish(h, state):
        scale = outward[:, h : h + 1]
        dk = dk_part_ref[:, cols(h)] + scale * mm(v_ref[:, cols(h)], state, 1, 1)
        dv = dv_part_ref[:, cols(h)] + scale * mm(k_ref[:, cols(h)], state, 1, 0)
        dk_ref[:, cols(h)] = dk.astype(BF16)
        dv_ref[:, cols(h)] = dv.astype(BF16)
        for place, (src, dst) in enumerate(((dk_ref, dk_hbm), (dv_ref, dv_hbm))):
            copy = pltpu.make_async_copy(
                src.at[:, cols(h)], dst.at[:, cols(h)], column_sem.at[place, h]
            )
            copy.start()
            stores.append(copy)

    scan(1, backward_state, inside, finish)

    for copy in stores:
        copy.wait()
    through_copy.wait_send()
    for copy in sum_copies:
        copy.wait_send()
    for way in range(2):
        for h in range(heads):
            exchange(way, h).wait_send()

        @pl.when(has_next(way))
        def _():
            for h in range(heads):
                for p in range(parts):
                    chain(way, h, p).wait_send()


def store(*refs):
    sem = refs[-1]
    copies = [pltpu.make_async_copy(refs[i], refs[4 + i], sem.at[i]) for i in range(4)]
    for copy in copies:
        copy.start()
    for copy in copies:
        copy.wait()


def local(queries, key_vectors, values, decay_log, doc_starts, gate_logits, norm_gain, grad_out):
    n_seq = lax.axis_size("seq")
    n_head = lax.axis_size("head")
    tokens, width = queries.shape
    heads = width // HEAD_DIM
    hbm = pl.BlockSpec(memory_space=pltpu.HBM)
    parts = 2
    states = (2, heads, HEAD_DIM, HEAD_DIM)
    out = jax.ShapeDtypeStruct((tokens, width), BF16)
    results = pl.pallas_call(
        functools.partial(kernel, n_seq, n_head, parts),
        out_shape=(out, out, out, out),
        in_specs=[hbm] * 8,
        out_specs=(hbm, hbm, hbm, hbm),
        scratch_shapes=[
            pltpu.VMEM((tokens, width), BF16),
            pltpu.VMEM((tokens, width), BF16),
            pltpu.VMEM((tokens, width), BF16),
            pltpu.VMEM((tokens, width), BF16),
            pltpu.VMEM((tokens, width), BF16),
            pltpu.VMEM((tokens, width), BF16),
            pltpu.VMEM((tokens, width), BF16),
            pltpu.VMEM(decay_log.shape, F32),
            pltpu.SMEM(doc_starts.shape, jnp.int32),
            pltpu.VMEM((tokens, width), BF16),
            pltpu.VMEM((1, width), F32),
            pltpu.VMEM((tokens, width), BF16),
            pltpu.VMEM(states, F32),
            pltpu.VMEM(states, F32),
            pltpu.VMEM(states, F32),
            pltpu.VMEM(states, F32),
            pltpu.VMEM(states, F32),
            pltpu.VMEM((2, heads, HEAD_DIM), F32),
            pltpu.VMEM((heads, HEAD_DIM, HEAD_DIM), BF16),
            pltpu.VMEM((heads, tokens, tokens), F32),
            pltpu.VMEM((heads, tokens, tokens), BF16),
            pltpu.VMEM((tokens, width), F32),
            pltpu.VMEM((tokens, width), F32),
            pltpu.VMEM((tokens, width), F32),
            pltpu.VMEM((tokens, width), BF16),
            pltpu.VMEM((tokens, width), F32),
            pltpu.VMEM((tokens, width), F32),
            pltpu.VMEM((tokens, tokens), F32),
            pltpu.VMEM((n_head, 8, tokens), F32),
            pltpu.SemaphoreType.DMA((8,)),
            pltpu.SemaphoreType.DMA((2,)),
            pltpu.SemaphoreType.DMA((2, heads)),
            pltpu.SemaphoreType.DMA((2, heads)),
            pltpu.SemaphoreType.DMA((2, heads)),
            pltpu.SemaphoreType.DMA((2, heads * parts)),
            pltpu.SemaphoreType.DMA((2, heads * parts)),
            pltpu.SemaphoreType.DMA((2,)),
            pltpu.SemaphoreType.DMA((max(n_head - 1, 1),)),
            pltpu.SemaphoreType.DMA((max(n_head - 1, 1),)),
        ],
        compiler_params=pltpu.CompilerParams(
            collective_id=0, has_side_effects=True, vmem_limit_bytes=VMEM_BYTES
        ),
        name="attention_both_ways",
    )(
        queries,
        key_vectors,
        values,
        decay_log,
        doc_starts,
        gate_logits,
        norm_gain.reshape(1, width),
        grad_out,
    )
    return pl.pallas_call(
        store,
        out_shape=(out, out, out, out),
        in_specs=[hbm] * 4,
        out_specs=(hbm, hbm, hbm, hbm),
        scratch_shapes=[pltpu.SemaphoreType.DMA((4,))],
        compiler_params=pltpu.CompilerParams(vmem_limit_bytes=VMEM_BYTES),
        name="store_results",
    )(*results)


def solution(mesh):
    placed = (
        P("seq", "head"),
        P("seq", "head"),
        P("seq", "head"),
        P("head", "seq"),
        P("seq", None),
        P("seq", "head"),
        P("head"),
        P("seq", "head"),
    )
    return jax.shard_map(
        local,
        mesh=mesh,
        in_specs=placed,
        out_specs=(P("seq", "head"), P("seq", "head"), P("seq", "head"), P("seq", "head")),
        check_vma=False,
    )
```

```python
import functools

import jax
import jax.numpy as jnp
from jax import lax
from jax.experimental import pallas as pl
from jax.experimental.pallas import tpu as pltpu
from jax.sharding import PartitionSpec as P

HEAD_DIM = 128
EPSILON = 1e-06
VMEM_BYTES = 60 * 1024 * 1024
MESH = pl.DeviceIdType.MESH
F32 = jnp.float32
BF16 = jnp.bfloat16
HIGHEST = lax.Precision.HIGHEST


def mm(a, b, ca, cb, precision=None):
    return lax.dot_general(
        a, b, (((ca,), (cb,)), ((), ())), precision=precision, preferred_element_type=F32
    )


def kernel(
    n_seq,
    n_head,
    parts,
    q_hbm,
    k_hbm,
    v_hbm,
    decay_hbm,
    starts_hbm,
    gate_hbm,
    gain_hbm,
    gout_hbm,
    dq_hbm,
    dk_hbm,
    dv_hbm,
    dgate_hbm,
    dq_ref,
    dk_ref,
    dv_ref,
    dgate_ref,
    q_ref,
    k_ref,
    v_ref,
    decay_ref,
    starts_ref,
    gate_ref,
    gain_ref,
    gout_ref,
    mine_ref,
    cross_ref,
    theirs_ref,
    onward_ref,
    inbound_ref,
    through_ref,
    enter_ref,
    weight_ref,
    mixing_ref,
    attended_ref,
    dnormed_ref,
    dgate_part_ref,
    qscaled_ref,
    dk_part_ref,
    dv_part_ref,
    bias_ref,
    sums_ref,
    load_sem,
    whole_sem,
    column_sem,
    state_send,
    state_recv,
    chain_send,
    chain_recv,
    through_sem,
    sums_send,
    sums_recv,
):
    tokens, width = q_ref.shape
    heads = width // HEAD_DIM
    features = width * n_head
    seq = lax.axis_index("seq")
    head = lax.axis_index("head")
    side = lax.rem(seq, 2)
    link = seq // 2
    links = n_seq // 2
    first = side == 0
    partner = seq + 1 - 2 * side

    loads = {}
    for place, (name, src, dst) in enumerate(
        (
            ("decay", decay_hbm, decay_ref),
            ("starts", starts_hbm, starts_ref),
            ("k", k_hbm, k_ref),
            ("v", v_hbm, v_ref),
            ("q", q_hbm, q_ref),
            ("gain", gain_hbm, gain_ref),
            ("gate", gate_hbm, gate_ref),
            ("gout", gout_hbm, gout_ref),
        )
    ):
        loads[name] = pltpu.make_async_copy(src, dst, load_sem.at[place])
        loads[name].start()

    def cols(h):
        return slice(h * HEAD_DIM, (h + 1) * HEAD_DIM)

    barrier = pltpu.get_barrier_semaphore()

    def greet(s, h):
        pl.semaphore_signal(barrier, inc=1, device_id={"seq": s, "head": h}, device_id_type=MESH)

    greet(partner, head)
    for d in range(1, n_head):
        greet(seq, lax.rem(head + d, n_head))

    @pl.when(link > 0)
    def _():
        greet(seq - 2, head)

    @pl.when(link < links - 1)
    def _():
        greet(seq + 2, head)

    def remote(src, dst, send, recv, s, h):
        return pltpu.make_async_remote_copy(
            src_ref=src,
            dst_ref=dst,
            send_sem=send,
            recv_sem=recv,
            device_id={"seq": s, "head": h},
            device_id_type=MESH,
        )

    through_copy = remote(
        through_ref.at[0], through_ref.at[1], through_sem.at[0], through_sem.at[1], partner, head
    )

    early = heads // 2
    part_rows = HEAD_DIM // parts

    def rows(p):
        return slice(p * part_rows, (p + 1) * part_rows)

    def exchange(way, h):
        source = mine_ref if h < early else cross_ref
        return remote(
            source.at[way, h],
            theirs_ref.at[way, h],
            state_send.at[way, h],
            state_recv.at[way, h],
            partner,
            head,
        )

    def chain(way, h, p):
        return remote(
            onward_ref.at[way, h, pl.ds(p * part_rows, part_rows)],
            inbound_ref.at[way, h, pl.ds(p * part_rows, part_rows)],
            chain_send.at[way, h * parts + p],
            chain_recv.at[way, h * parts + p],
            seq + 2 if way == 0 else seq - 2,
            head,
        )

    def has_next(way):
        return link < links - 1 if way == 0 else link > 0

    def has_previous(way):
        return link > 0 if way == 0 else link < links - 1

    def leads(way):
        return first if way == 0 else jnp.logical_not(first)

    def throughs(h):
        return through_ref[0, h : h + 1, :], through_ref[1, h : h + 1, :]

    def pair_then_chain(way, h):
        exchange(way, h).wait_recv()
        t_mine, t_theirs = throughs(h)
        state = []
        for p in range(parts):
            theirs = theirs_ref[way, h, rows(p)]
            pair = (
                jnp.where(leads(way), t_theirs, 1.0) * mine_ref[way, h, rows(p)]
                + jnp.where(leads(way), 1.0, t_mine) * theirs
            )

            @pl.when(has_previous(way))
            def _():
                chain(way, h, p).wait_recv()

            arrived = inbound_ref[way, h, rows(p)]

            @pl.when(has_next(way))
            def _():
                onward_ref[way, h, rows(p)] = t_mine * t_theirs * arrived + pair
                chain(way, h, p).start()

            state.append(
                jnp.where(leads(way), 1.0, t_theirs) * arrived
                + jnp.where(leads(way), 0.0, 1.0) * theirs
            )
        return jnp.concatenate(state, axis=0)

    def chain_alone(way, h):
        t_mine, t_theirs = throughs(h)
        for p in range(parts):
            mine = mine_ref[way, h, rows(p)]

            @pl.when(has_previous(way))
            def _():
                chain(way, h, p).wait_recv()

            arrived = inbound_ref[way, h, rows(p)]

            @pl.when(has_next(way))
            def _():
                onward_ref[way, h, rows(p)] = (
                    t_mine * t_theirs * arrived + jnp.where(leads(way), t_theirs, 1.0) * mine
                )
                chain(way, h, p).start()

            cross_ref[way, h, rows(p)] = (
                jnp.where(leads(way), t_mine, 1.0) * arrived
                + jnp.where(leads(way), 1.0, 0.0) * mine
            )
        exchange(way, h).start()

    def pair_last(way, h):
        exchange(way, h).wait_recv()
        _, t_theirs = throughs(h)
        return jnp.where(leads(way), 1.0, t_theirs) * inbound_ref[way, h] + theirs_ref[way, h]

    def scan(way, local_state, work, use):
        pairs = [h for i in range(early) for h in (i, early + i)] + list(range(2 * early, heads))
        for h in pairs:
            mine_ref[way, h] = local_state(h)
            if h < early:
                exchange(way, h).start()
            else:
                if way == 0 and h == early:
                    through_copy.wait_recv()

                @pl.when(jnp.logical_not(has_previous(way)))
                def _():
                    chain_alone(way, h)

        later = list(range(heads))
        later = later[early:] + later[:early]
        ready = 0
        for ready in range(2):
            work(later[ready])
        ready = 2
        for h in range(early, heads):

            @pl.when(has_previous(way))
            def _():
                chain_alone(way, h)

            if ready < heads:
                work(later[ready])
                ready += 1
        for h in pairs:
            if h < early:
                state = pair_then_chain(way, h)
            else:
                state = pair_last(way, h)
            while ready <= later.index(h):
                work(later[ready])
                ready += 1
            use(h, state.astype(BF16))
            if ready < heads:
                work(later[ready])
                ready += 1

    for way in range(2):

        @pl.when(jnp.logical_not(has_previous(way)))
        def _():
            inbound_ref[way] = jnp.zeros(inbound_ref.shape[1:], F32)

    row_ids = lax.broadcasted_iota(jnp.int32, (tokens, tokens), 0)
    col_ids = lax.broadcasted_iota(jnp.int32, (tokens, tokens), 1)
    causal = row_ids >= col_ids
    lower = causal.astype(F32)
    loads["decay"].wait()
    loads["starts"].wait()
    decay = decay_ref[...]
    latest = jnp.int32(0)
    for j in range(starts_ref.shape[1]):
        latest += (starts_ref[0, j] < tokens).astype(jnp.int32)
    through = jnp.where(latest == 0, jnp.exp(jnp.sum(decay, axis=1, keepdims=True)), 0.0)
    through_ref[0] = jnp.broadcast_to(through, (heads, HEAD_DIM))
    pl.semaphore_wait(
        barrier,
        n_head + (link > 0).astype(jnp.int32) + (link < links - 1).astype(jnp.int32),
    )
    through_copy.start()
    sum_col = mm(lower, decay, 1, 1, HIGHEST)
    sum_row = mm(decay, lower, 1, 1, HIGHEST)
    ids_col = lax.broadcasted_iota(jnp.int32, (tokens, 1), 0)
    ids_row = lax.broadcasted_iota(jnp.int32, (1, tokens), 1)
    count_col = jnp.zeros((tokens, 1), jnp.int32)
    count_row = jnp.zeros((1, tokens), jnp.int32)
    for j in range(starts_ref.shape[1]):
        start = starts_ref[0, j]
        count_col += (ids_col >= start).astype(jnp.int32)
        count_row += (ids_row >= start).astype(jnp.int32)
    outward = jnp.where(
        count_col == latest, jnp.exp(sum_col[tokens - 1 : tokens, :] - sum_col), 0.0
    )
    inward = jnp.where(count_col == 0, jnp.exp(sum_col), 0.0)
    keep = jnp.logical_and(causal, count_col == count_row)
    bias_ref[...] = jnp.where(keep, 0.0, -1e30)
    loads["k"].wait()
    loads["v"].wait()

    def forward_state(h):
        scaled = (k_ref[:, cols(h)].astype(F32) * outward[:, h : h + 1]).astype(BF16)
        return mm(scaled, v_ref[:, cols(h)], 0, 0)

    def within(h):
        q = q_ref[:, cols(h)]
        weight = jnp.exp(sum_col[:, h : h + 1] - sum_row[h : h + 1, :] + bias_ref[...])
        weight_ref[h] = weight
        mixing = (weight * mm(q, k_ref[:, cols(h)], 1, 1)).astype(BF16)
        mixing_ref[h] = mixing
        attended_ref[:, cols(h)] = mm(mixing, v_ref[:, cols(h)], 1, 0)
        qscaled_ref[:, cols(h)] = (q.astype(F32) * inward[:, h : h + 1]).astype(BF16)
        opening = jax.nn.sigmoid(gate_ref[:, cols(h)].astype(F32))
        dnormed = gout_ref[:, cols(h)].astype(F32) * gain_ref[:, cols(h)] * opening
        dnormed_ref[:, cols(h)] = dnormed
        dgate_part_ref[:, cols(h)] = dnormed * (1.0 - opening)

    sums = [jnp.zeros((tokens, HEAD_DIM), F32)] * 2

    def attend(h, state):
        enter_ref[h] = state
        attended = attended_ref[:, cols(h)] + inward[:, h : h + 1] * mm(
            q_ref[:, cols(h)], state, 1, 0
        )
        attended_ref[:, cols(h)] = attended
        sums[0] += attended * attended
        sums[1] += dnormed_ref[:, cols(h)] * attended

    waited = []

    def first_work(h):
        if not waited:
            for name in ("q", "gain", "gate", "gout"):
                loads[name].wait()
            waited.append(True)
        within(h)

    scan(0, forward_state, first_work, attend)
    squares, products = sums

    ones = jnp.ones((8, HEAD_DIM), F32)
    square_rows = mm(ones, squares, 1, 1, HIGHEST)
    product_rows = mm(ones, products, 1, 1, HIGHEST)
    sum_ids = lax.broadcasted_iota(jnp.int32, (8, tokens), 0)
    sums_ref[0] = jnp.where(sum_ids == 0, square_rows, product_rows)
    sum_copies = [
        remote(
            sums_ref.at[0],
            sums_ref.at[d],
            sums_send.at[d - 1],
            sums_recv.at[d - 1],
            seq,
            lax.rem(head + d, n_head),
        )
        for d in range(1, n_head)
    ]
    for copy in sum_copies:
        copy.start()
    for copy in sum_copies:
        copy.wait_recv()
    totals = sums_ref[0]
    for d in range(1, n_head):
        totals += sums_ref[d]
    totals = totals / features
    inverse = lax.rsqrt(totals[0:1] + EPSILON)
    pull = totals[1:2] * inverse * inverse * inverse
    scalars = jnp.where(sum_ids == 0, inverse, pull)
    unit = (
        lax.broadcasted_iota(jnp.int32, (8, 8), 0) == lax.broadcasted_iota(jnp.int32, (8, 8), 1)
    ).astype(F32)
    scalars = mm(scalars, unit, 0, 0, HIGHEST)
    inverse = scalars[:, 0:1]
    pull = scalars[:, 1:2]

    grads = {}

    def backward_state(h):
        grad = (dnormed_ref[:, cols(h)] * inverse - attended_ref[:, cols(h)] * pull).astype(BF16)
        grads[h] = grad
        return mm(qscaled_ref[:, cols(h)], grad, 0, 0)

    stores = []
    worked = []

    def inside(h):
        q = q_ref[:, cols(h)]
        k = k_ref[:, cols(h)]
        v = v_ref[:, cols(h)]
        grad = grads[h]
        grad_mixing = (weight_ref[h] * mm(grad, v, 1, 1)).astype(BF16)
        dq = mm(grad_mixing, k, 1, 0) + inward[:, h : h + 1] * mm(grad, enter_ref[h], 1, 1)
        dq_ref[:, cols(h)] = dq.astype(BF16)
        dk_part_ref[:, cols(h)] = mm(grad_mixing, q, 0, 0)
        dv_part_ref[:, cols(h)] = mm(mixing_ref[h], grad, 0, 0)
        dgate_ref[:, cols(h)] = (
            dgate_part_ref[:, cols(h)] * attended_ref[:, cols(h)] * inverse
        ).astype(BF16)
        worked.append(h)
        if len(worked) == heads:
            for place, (src, dst) in enumerate(((dq_ref, dq_hbm), (dgate_ref, dgate_hbm))):
                copy = pltpu.make_async_copy(src, dst, whole_sem.at[place])
                copy.start()
                stores.append(copy)

    def finish(h, state):
        scale = outward[:, h : h + 1]
        dk = dk_part_ref[:, cols(h)] + scale * mm(v_ref[:, cols(h)], state, 1, 1)
        dv = dv_part_ref[:, cols(h)] + scale * mm(k_ref[:, cols(h)], state, 1, 0)
        dk_ref[:, cols(h)] = dk.astype(BF16)
        dv_ref[:, cols(h)] = dv.astype(BF16)
        for place, (src, dst) in enumerate(((dk_ref, dk_hbm), (dv_ref, dv_hbm))):
            copy = pltpu.make_async_copy(
                src.at[:, cols(h)], dst.at[:, cols(h)], column_sem.at[place, h]
            )
            copy.start()
            stores.append(copy)

    scan(1, backward_state, inside, finish)

    for copy in stores:
        copy.wait()
    through_copy.wait_send()
    for copy in sum_copies:
        copy.wait_send()
    for way in range(2):
        for h in range(heads):
            exchange(way, h).wait_send()

        @pl.when(has_next(way))
        def _():
            for h in range(heads):
                for p in range(parts):
                    chain(way, h, p).wait_send()


def store(*refs):
    held, sem = refs[8:12], refs[12]
    loads = [pltpu.make_async_copy(refs[i], held[i], sem.at[i]) for i in range(4)]
    stores = [pltpu.make_async_copy(held[i], refs[4 + i], sem.at[4 + i]) for i in range(4)]
    for load in loads:
        load.start()
    for i in range(4):
        loads[i].wait()
        stores[i].start()
    for copy in stores:
        copy.wait()


def local(queries, key_vectors, values, decay_log, doc_starts, gate_logits, norm_gain, grad_out):
    n_seq = lax.axis_size("seq")
    n_head = lax.axis_size("head")
    tokens, width = queries.shape
    heads = width // HEAD_DIM
    hbm = pl.BlockSpec(memory_space=pltpu.HBM)
    parts = 2
    states = (2, heads, HEAD_DIM, HEAD_DIM)
    out = jax.ShapeDtypeStruct((tokens, width), BF16)
    results = pl.pallas_call(
        functools.partial(kernel, n_seq, n_head, parts),
        out_shape=(out, out, out, out),
        in_specs=[hbm] * 8,
        out_specs=(hbm, hbm, hbm, hbm),
        scratch_shapes=[
            pltpu.VMEM((tokens, width), BF16),
            pltpu.VMEM((tokens, width), BF16),
            pltpu.VMEM((tokens, width), BF16),
            pltpu.VMEM((tokens, width), BF16),
            pltpu.VMEM((tokens, width), BF16),
            pltpu.VMEM((tokens, width), BF16),
            pltpu.VMEM((tokens, width), BF16),
            pltpu.VMEM(decay_log.shape, F32),
            pltpu.SMEM(doc_starts.shape, jnp.int32),
            pltpu.VMEM((tokens, width), BF16),
            pltpu.VMEM((1, width), F32),
            pltpu.VMEM((tokens, width), BF16),
            pltpu.VMEM(states, F32),
            pltpu.VMEM(states, F32),
            pltpu.VMEM(states, F32),
            pltpu.VMEM(states, F32),
            pltpu.VMEM(states, F32),
            pltpu.VMEM((2, heads, HEAD_DIM), F32),
            pltpu.VMEM((heads, HEAD_DIM, HEAD_DIM), BF16),
            pltpu.VMEM((heads, tokens, tokens), F32),
            pltpu.VMEM((heads, tokens, tokens), BF16),
            pltpu.VMEM((tokens, width), F32),
            pltpu.VMEM((tokens, width), F32),
            pltpu.VMEM((tokens, width), F32),
            pltpu.VMEM((tokens, width), BF16),
            pltpu.VMEM((tokens, width), F32),
            pltpu.VMEM((tokens, width), F32),
            pltpu.VMEM((tokens, tokens), F32),
            pltpu.VMEM((n_head, 8, tokens), F32),
            pltpu.SemaphoreType.DMA((8,)),
            pltpu.SemaphoreType.DMA((2,)),
            pltpu.SemaphoreType.DMA((2, heads)),
            pltpu.SemaphoreType.DMA((2, heads)),
            pltpu.SemaphoreType.DMA((2, heads)),
            pltpu.SemaphoreType.DMA((2, heads * parts)),
            pltpu.SemaphoreType.DMA((2, heads * parts)),
            pltpu.SemaphoreType.DMA((2,)),
            pltpu.SemaphoreType.DMA((max(n_head - 1, 1),)),
            pltpu.SemaphoreType.DMA((max(n_head - 1, 1),)),
        ],
        compiler_params=pltpu.CompilerParams(
            collective_id=0, has_side_effects=True, vmem_limit_bytes=VMEM_BYTES
        ),
        name="attention_both_ways",
    )(
        queries,
        key_vectors,
        values,
        decay_log,
        doc_starts,
        gate_logits,
        norm_gain.reshape(1, width),
        grad_out,
    )
    return pl.pallas_call(
        store,
        out_shape=(out, out, out, out),
        in_specs=[hbm] * 4,
        out_specs=(hbm, hbm, hbm, hbm),
        scratch_shapes=[pltpu.VMEM((tokens, width), BF16)] * 4 + [pltpu.SemaphoreType.DMA((8,))],
        compiler_params=pltpu.CompilerParams(vmem_limit_bytes=VMEM_BYTES),
        name="store_results",
    )(*results)


def solution(mesh):
    placed = (
        P("seq", "head"),
        P("seq", "head"),
        P("seq", "head"),
        P("head", "seq"),
        P("seq", None),
        P("seq", "head"),
        P("head"),
        P("seq", "head"),
    )
    return jax.shard_map(
        local,
        mesh=mesh,
        in_specs=placed,
        out_specs=(P("seq", "head"), P("seq", "head"), P("seq", "head"), P("seq", "head")),
        check_vma=False,
    )
```

```python
import functools

import jax
import jax.numpy as jnp
from jax import lax
from jax.experimental import pallas as pl
from jax.experimental.pallas import tpu as pltpu
from jax.sharding import PartitionSpec as P

HEAD_DIM = 128
EPSILON = 1e-06
VMEM_BYTES = 60 * 1024 * 1024
MESH = pl.DeviceIdType.MESH
F32 = jnp.float32
BF16 = jnp.bfloat16
HIGHEST = lax.Precision.HIGHEST


def mm(a, b, ca, cb, precision=None):
    return lax.dot_general(
        a, b, (((ca,), (cb,)), ((), ())), precision=precision, preferred_element_type=F32
    )


def kernel(
    n_seq,
    n_head,
    parts,
    q_hbm,
    k_hbm,
    v_hbm,
    decay_hbm,
    starts_hbm,
    gate_hbm,
    gain_hbm,
    gout_hbm,
    dq_hbm,
    dk_hbm,
    dv_hbm,
    dgate_hbm,
    dq_ref,
    dk_ref,
    dv_ref,
    dgate_ref,
    q_ref,
    k_ref,
    v_ref,
    decay_ref,
    starts_ref,
    gate_ref,
    gain_ref,
    gout_ref,
    mine_ref,
    cross_ref,
    theirs_ref,
    onward_ref,
    inbound_ref,
    through_ref,
    enter_ref,
    weight_ref,
    mixing_ref,
    attended_ref,
    dnormed_ref,
    dgate_part_ref,
    qscaled_ref,
    dk_part_ref,
    dv_part_ref,
    bias_ref,
    sums_ref,
    load_sem,
    whole_sem,
    column_sem,
    state_send,
    state_recv,
    chain_send,
    chain_recv,
    through_sem,
    sums_send,
    sums_recv,
):
    tokens, width = q_ref.shape
    heads = width // HEAD_DIM
    features = width * n_head
    seq = lax.axis_index("seq")
    head = lax.axis_index("head")
    side = lax.rem(seq, 2)
    link = seq // 2
    links = n_seq // 2
    first = side == 0
    partner = seq + 1 - 2 * side

    loads = {}
    for place, (name, src, dst) in enumerate(
        (
            ("decay", decay_hbm, decay_ref),
            ("starts", starts_hbm, starts_ref),
            ("k", k_hbm, k_ref),
            ("v", v_hbm, v_ref),
            ("q", q_hbm, q_ref),
            ("gain", gain_hbm, gain_ref),
            ("gate", gate_hbm, gate_ref),
            ("gout", gout_hbm, gout_ref),
        )
    ):
        loads[name] = pltpu.make_async_copy(src, dst, load_sem.at[place])
        loads[name].start()

    def cols(h):
        return slice(h * HEAD_DIM, (h + 1) * HEAD_DIM)

    barrier = pltpu.get_barrier_semaphore()

    def greet(s, h):
        pl.semaphore_signal(barrier, inc=1, device_id={"seq": s, "head": h}, device_id_type=MESH)

    greet(partner, head)
    for d in range(1, n_head):
        greet(seq, lax.rem(head + d, n_head))

    @pl.when(link > 0)
    def _():
        greet(seq - 2, head)

    @pl.when(link < links - 1)
    def _():
        greet(seq + 2, head)

    def remote(src, dst, send, recv, s, h):
        return pltpu.make_async_remote_copy(
            src_ref=src,
            dst_ref=dst,
            send_sem=send,
            recv_sem=recv,
            device_id={"seq": s, "head": h},
            device_id_type=MESH,
        )

    through_copy = remote(
        through_ref.at[0], through_ref.at[1], through_sem.at[0], through_sem.at[1], partner, head
    )

    early = heads // 2
    part_rows = HEAD_DIM // parts

    def rows(p):
        return slice(p * part_rows, (p + 1) * part_rows)

    def exchange(way, h):
        source = mine_ref if h < early else cross_ref
        return remote(
            source.at[way, h],
            theirs_ref.at[way, h],
            state_send.at[way, h],
            state_recv.at[way, h],
            partner,
            head,
        )

    def chain(way, h, p):
        return remote(
            onward_ref.at[way, h, pl.ds(p * part_rows, part_rows)],
            inbound_ref.at[way, h, pl.ds(p * part_rows, part_rows)],
            chain_send.at[way, h * parts + p],
            chain_recv.at[way, h * parts + p],
            seq + 2 if way == 0 else seq - 2,
            head,
        )

    def has_next(way):
        return link < links - 1 if way == 0 else link > 0

    def has_previous(way):
        return link > 0 if way == 0 else link < links - 1

    def leads(way):
        return first if way == 0 else jnp.logical_not(first)

    def throughs(h):
        return through_ref[0, h : h + 1, :], through_ref[1, h : h + 1, :]

    def pair_then_chain(way, h):
        exchange(way, h).wait_recv()
        t_mine, t_theirs = throughs(h)
        state = []
        for p in range(parts):
            theirs = theirs_ref[way, h, rows(p)]
            pair = (
                jnp.where(leads(way), t_theirs, 1.0) * mine_ref[way, h, rows(p)]
                + jnp.where(leads(way), 1.0, t_mine) * theirs
            )

            @pl.when(has_previous(way))
            def _():
                chain(way, h, p).wait_recv()

            arrived = inbound_ref[way, h, rows(p)]

            @pl.when(has_next(way))
            def _():
                onward_ref[way, h, rows(p)] = t_mine * t_theirs * arrived + pair
                chain(way, h, p).start()

            state.append(
                jnp.where(leads(way), 1.0, t_theirs) * arrived
                + jnp.where(leads(way), 0.0, 1.0) * theirs
            )
        return jnp.concatenate(state, axis=0)

    def chain_alone(way, h):
        t_mine, t_theirs = throughs(h)
        for p in range(parts):
            mine = mine_ref[way, h, rows(p)]

            @pl.when(has_previous(way))
            def _():
                chain(way, h, p).wait_recv()

            arrived = inbound_ref[way, h, rows(p)]

            @pl.when(has_next(way))
            def _():
                onward_ref[way, h, rows(p)] = (
                    t_mine * t_theirs * arrived + jnp.where(leads(way), t_theirs, 1.0) * mine
                )
                chain(way, h, p).start()

            cross_ref[way, h, rows(p)] = (
                jnp.where(leads(way), t_mine, 1.0) * arrived
                + jnp.where(leads(way), 1.0, 0.0) * mine
            )
        exchange(way, h).start()

    def pair_last(way, h):
        exchange(way, h).wait_recv()
        _, t_theirs = throughs(h)
        return jnp.where(leads(way), 1.0, t_theirs) * inbound_ref[way, h] + theirs_ref[way, h]

    def scan(way, local_state, work, use):
        pairs = [h for i in range(early) for h in (i, early + i)] + list(range(2 * early, heads))
        for h in pairs:
            mine_ref[way, h] = local_state(h)
            if h < early:
                exchange(way, h).start()
            else:
                if way == 0 and h == early:
                    through_copy.wait_recv()

                @pl.when(jnp.logical_not(has_previous(way)))
                def _():
                    chain_alone(way, h)

        later = list(range(heads))
        later = later[early:] + later[:early]
        ready = 0
        for ready in range(2):
            work(later[ready])
        ready = 2
        for h in range(early, heads):

            @pl.when(has_previous(way))
            def _():
                chain_alone(way, h)

            if ready < heads:
                work(later[ready])
                ready += 1
        for h in pairs:
            if h < early:
                state = pair_then_chain(way, h)
            else:
                state = pair_last(way, h)
            while ready <= later.index(h):
                work(later[ready])
                ready += 1
            use(h, state.astype(BF16))
            if ready < heads:
                work(later[ready])
                ready += 1

    for way in range(2):

        @pl.when(jnp.logical_not(has_previous(way)))
        def _():
            inbound_ref[way] = jnp.zeros(inbound_ref.shape[1:], F32)

    row_ids = lax.broadcasted_iota(jnp.int32, (tokens, tokens), 0)
    col_ids = lax.broadcasted_iota(jnp.int32, (tokens, tokens), 1)
    causal = row_ids >= col_ids
    lower = causal.astype(F32)
    loads["decay"].wait()
    loads["starts"].wait()
    decay = decay_ref[...]
    latest = jnp.int32(0)
    for j in range(starts_ref.shape[1]):
        latest += (starts_ref[0, j] < tokens).astype(jnp.int32)
    through = jnp.where(latest == 0, jnp.exp(jnp.sum(decay, axis=1, keepdims=True)), 0.0)
    through_ref[0] = jnp.broadcast_to(through, (heads, HEAD_DIM))
    pl.semaphore_wait(
        barrier,
        n_head + (link > 0).astype(jnp.int32) + (link < links - 1).astype(jnp.int32),
    )
    through_copy.start()
    sum_col = mm(lower, decay, 1, 1, HIGHEST)
    sum_row = mm(decay, lower, 1, 1, HIGHEST)
    ids_col = lax.broadcasted_iota(jnp.int32, (tokens, 1), 0)
    ids_row = lax.broadcasted_iota(jnp.int32, (1, tokens), 1)
    count_col = jnp.zeros((tokens, 1), jnp.int32)
    count_row = jnp.zeros((1, tokens), jnp.int32)
    for j in range(starts_ref.shape[1]):
        start = starts_ref[0, j]
        count_col += (ids_col >= start).astype(jnp.int32)
        count_row += (ids_row >= start).astype(jnp.int32)
    outward = jnp.where(
        count_col == latest, jnp.exp(sum_col[tokens - 1 : tokens, :] - sum_col), 0.0
    )
    inward = jnp.where(count_col == 0, jnp.exp(sum_col), 0.0)
    keep = jnp.logical_and(causal, count_col == count_row)
    bias_ref[...] = jnp.where(keep, 0.0, -1e30)
    loads["k"].wait()
    loads["v"].wait()

    def forward_state(h):
        scaled = (k_ref[:, cols(h)].astype(F32) * outward[:, h : h + 1]).astype(BF16)
        return mm(scaled, v_ref[:, cols(h)], 0, 0)

    def within(h):
        q = q_ref[:, cols(h)]
        weight = jnp.exp(sum_col[:, h : h + 1] - sum_row[h : h + 1, :] + bias_ref[...])
        weight_ref[h] = weight
        mixing = (weight * mm(q, k_ref[:, cols(h)], 1, 1)).astype(BF16)
        mixing_ref[h] = mixing
        attended_ref[:, cols(h)] = mm(mixing, v_ref[:, cols(h)], 1, 0)
        qscaled_ref[:, cols(h)] = (q.astype(F32) * inward[:, h : h + 1]).astype(BF16)
        opening = jax.nn.sigmoid(gate_ref[:, cols(h)].astype(F32))
        dnormed = gout_ref[:, cols(h)].astype(F32) * gain_ref[:, cols(h)] * opening
        dnormed_ref[:, cols(h)] = dnormed
        dgate_part_ref[:, cols(h)] = dnormed * (1.0 - opening)

    sums = [jnp.zeros((tokens, HEAD_DIM), F32)] * 2

    def attend(h, state):
        enter_ref[h] = state
        attended = attended_ref[:, cols(h)] + inward[:, h : h + 1] * mm(
            q_ref[:, cols(h)], state, 1, 0
        )
        attended_ref[:, cols(h)] = attended
        sums[0] += attended * attended
        sums[1] += dnormed_ref[:, cols(h)] * attended

    waited = []

    def first_work(h):
        if not waited:
            for name in ("q", "gain", "gate", "gout"):
                loads[name].wait()
            waited.append(True)
        within(h)

    scan(0, forward_state, first_work, attend)
    squares, products = sums

    ones = jnp.ones((8, HEAD_DIM), F32)
    square_rows = mm(ones, squares, 1, 1, HIGHEST)
    product_rows = mm(ones, products, 1, 1, HIGHEST)
    sum_ids = lax.broadcasted_iota(jnp.int32, (8, tokens), 0)
    sums_ref[0] = jnp.where(sum_ids == 0, square_rows, product_rows)
    sum_copies = [
        remote(
            sums_ref.at[0],
            sums_ref.at[d],
            sums_send.at[d - 1],
            sums_recv.at[d - 1],
            seq,
            lax.rem(head + d, n_head),
        )
        for d in range(1, n_head)
    ]
    for copy in sum_copies:
        copy.start()
    for copy in sum_copies:
        copy.wait_recv()
    totals = sums_ref[0]
    for d in range(1, n_head):
        totals += sums_ref[d]
    totals = totals / features
    inverse = lax.rsqrt(totals[0:1] + EPSILON)
    pull = totals[1:2] * inverse * inverse * inverse
    scalars = jnp.where(sum_ids == 0, inverse, pull)
    unit = (
        lax.broadcasted_iota(jnp.int32, (8, 8), 0) == lax.broadcasted_iota(jnp.int32, (8, 8), 1)
    ).astype(F32)
    scalars = mm(scalars, unit, 0, 0, HIGHEST)
    inverse = scalars[:, 0:1]
    pull = scalars[:, 1:2]

    grads = {}

    def backward_state(h):
        grad = (dnormed_ref[:, cols(h)] * inverse - attended_ref[:, cols(h)] * pull).astype(BF16)
        grads[h] = grad
        return mm(qscaled_ref[:, cols(h)], grad, 0, 0)

    stores = []
    worked = []

    def inside(h):
        q = q_ref[:, cols(h)]
        k = k_ref[:, cols(h)]
        v = v_ref[:, cols(h)]
        grad = grads[h]
        grad_mixing = (weight_ref[h] * mm(grad, v, 1, 1)).astype(BF16)
        dq = mm(grad_mixing, k, 1, 0) + inward[:, h : h + 1] * mm(grad, enter_ref[h], 1, 1)
        dq_ref[:, cols(h)] = dq.astype(BF16)
        dk_part_ref[:, cols(h)] = mm(grad_mixing, q, 0, 0)
        dv_part_ref[:, cols(h)] = mm(mixing_ref[h], grad, 0, 0)
        dgate_ref[:, cols(h)] = (
            dgate_part_ref[:, cols(h)] * attended_ref[:, cols(h)] * inverse
        ).astype(BF16)
        worked.append(h)
        if len(worked) == heads:
            for place, (src, dst) in enumerate(((dq_ref, dq_hbm), (dgate_ref, dgate_hbm))):
                copy = pltpu.make_async_copy(src, dst, whole_sem.at[place])
                copy.start()
                stores.append(copy)

    def finish(h, state):
        scale = outward[:, h : h + 1]
        dk = dk_part_ref[:, cols(h)] + scale * mm(v_ref[:, cols(h)], state, 1, 1)
        dv = dv_part_ref[:, cols(h)] + scale * mm(k_ref[:, cols(h)], state, 1, 0)
        dk_ref[:, cols(h)] = dk.astype(BF16)
        dv_ref[:, cols(h)] = dv.astype(BF16)
        for place, (src, dst) in enumerate(((dk_ref, dk_hbm), (dv_ref, dv_hbm))):
            copy = pltpu.make_async_copy(
                src.at[:, cols(h)], dst.at[:, cols(h)], column_sem.at[place, h]
            )
            copy.start()
            stores.append(copy)

    scan(1, backward_state, inside, finish)

    for copy in stores:
        copy.wait()
    through_copy.wait_send()
    for copy in sum_copies:
        copy.wait_send()
    for way in range(2):
        for h in range(heads):
            exchange(way, h).wait_send()

        @pl.when(has_next(way))
        def _():
            for h in range(heads):
                for p in range(parts):
                    chain(way, h, p).wait_send()


def store(*refs):
    held, sem = refs[8:12], refs[12]
    loads = [pltpu.make_async_copy(refs[i], held[i], sem.at[i]) for i in range(4)]
    stores = [pltpu.make_async_copy(held[i], refs[4 + i], sem.at[4 + i]) for i in range(4)]
    for load in loads:
        load.start()
    for i in range(4):
        loads[i].wait()
        stores[i].start()
    for copy in stores:
        copy.wait()


def local(queries, key_vectors, values, decay_log, doc_starts, gate_logits, norm_gain, grad_out):
    n_seq = lax.axis_size("seq")
    n_head = lax.axis_size("head")
    tokens, width = queries.shape
    heads = width // HEAD_DIM
    hbm = pl.BlockSpec(memory_space=pltpu.HBM)
    parts = 1
    states = (2, heads, HEAD_DIM, HEAD_DIM)
    out = jax.ShapeDtypeStruct((tokens, width), BF16)
    results = pl.pallas_call(
        functools.partial(kernel, n_seq, n_head, parts),
        out_shape=(out, out, out, out),
        in_specs=[hbm] * 8,
        out_specs=(hbm, hbm, hbm, hbm),
        scratch_shapes=[
            pltpu.VMEM((tokens, width), BF16),
            pltpu.VMEM((tokens, width), BF16),
            pltpu.VMEM((tokens, width), BF16),
            pltpu.VMEM((tokens, width), BF16),
            pltpu.VMEM((tokens, width), BF16),
            pltpu.VMEM((tokens, width), BF16),
            pltpu.VMEM((tokens, width), BF16),
            pltpu.VMEM(decay_log.shape, F32),
            pltpu.SMEM(doc_starts.shape, jnp.int32),
            pltpu.VMEM((tokens, width), BF16),
            pltpu.VMEM((1, width), F32),
            pltpu.VMEM((tokens, width), BF16),
            pltpu.VMEM(states, F32),
            pltpu.VMEM(states, F32),
            pltpu.VMEM(states, F32),
            pltpu.VMEM(states, F32),
            pltpu.VMEM(states, F32),
            pltpu.VMEM((2, heads, HEAD_DIM), F32),
            pltpu.VMEM((heads, HEAD_DIM, HEAD_DIM), BF16),
            pltpu.VMEM((heads, tokens, tokens), F32),
            pltpu.VMEM((heads, tokens, tokens), BF16),
            pltpu.VMEM((tokens, width), F32),
            pltpu.VMEM((tokens, width), F32),
            pltpu.VMEM((tokens, width), F32),
            pltpu.VMEM((tokens, width), BF16),
            pltpu.VMEM((tokens, width), F32),
            pltpu.VMEM((tokens, width), F32),
            pltpu.VMEM((tokens, tokens), F32),
            pltpu.VMEM((n_head, 8, tokens), F32),
            pltpu.SemaphoreType.DMA((8,)),
            pltpu.SemaphoreType.DMA((2,)),
            pltpu.SemaphoreType.DMA((2, heads)),
            pltpu.SemaphoreType.DMA((2, heads)),
            pltpu.SemaphoreType.DMA((2, heads)),
            pltpu.SemaphoreType.DMA((2, heads * parts)),
            pltpu.SemaphoreType.DMA((2, heads * parts)),
            pltpu.SemaphoreType.DMA((2,)),
            pltpu.SemaphoreType.DMA((max(n_head - 1, 1),)),
            pltpu.SemaphoreType.DMA((max(n_head - 1, 1),)),
        ],
        compiler_params=pltpu.CompilerParams(
            collective_id=0, has_side_effects=True, vmem_limit_bytes=VMEM_BYTES
        ),
        name="attention_both_ways",
    )(
        queries,
        key_vectors,
        values,
        decay_log,
        doc_starts,
        gate_logits,
        norm_gain.reshape(1, width),
        grad_out,
    )
    return pl.pallas_call(
        store,
        out_shape=(out, out, out, out),
        in_specs=[hbm] * 4,
        out_specs=(hbm, hbm, hbm, hbm),
        scratch_shapes=[pltpu.VMEM((tokens, width), BF16)] * 4 + [pltpu.SemaphoreType.DMA((8,))],
        compiler_params=pltpu.CompilerParams(vmem_limit_bytes=VMEM_BYTES),
        name="store_results",
    )(*results)


def solution(mesh):
    placed = (
        P("seq", "head"),
        P("seq", "head"),
        P("seq", "head"),
        P("head", "seq"),
        P("seq", None),
        P("seq", "head"),
        P("head"),
        P("seq", "head"),
    )
    return jax.shard_map(
        local,
        mesh=mesh,
        in_specs=placed,
        out_specs=(P("seq", "head"), P("seq", "head"), P("seq", "head"), P("seq", "head")),
        check_vma=False,
    )
```
